256 devices in a mesh: grp: 8 (over x_lo, y), tile: 32 (over x_hi, z, core).
Axes of the slice: x: 4 (x_hi: 2, x_lo: 2; x = x_hi * 2 + x_lo), y: 4, z: 8, core: 2. Of those that a mesh axis runs over, the one named last changes fastest.
Arguments:
- acts: bfloat16 [2048, 5120], P(('grp', 'tile')), may hold values from -6 to 6
- grads: bfloat16 [2048, 20480], P(('grp', 'tile')), may hold values from -6 to 6
- basis_in: bfloat16 [5120, 2560], P(None, 'tile'), may hold values from -0.078125 to 0.078125
- basis_out: bfloat16 [20480, 10240], P('grp', 'tile'), may hold values from -0.0390625 to 0.0390625
- tenant: int32 [8], replicated, may hold values from 0 to 1, as said below
Outputs:
- held_out: float32 [2, 10240, 2560], P(None, ('tile', 'grp'))
The draws below stay inside these ranges and needn't reach their ends.
Inputs may be any that keep to these rules, and one draw needn't show every extreme that they name: Each tenant owns exactly 4 of the sequences.
All inputs are finite; a program needn't handle non-finite values.
Results may differ from the reference program's by a relative error of at most 0.017.
Values may be sent and summed in bfloat16 or wider, within the bound.
No kernel may reach another device: no remote copies, remote signals or barrier semaphores. Data moves between devices by JAX's collectives and lax.ppermute only.
A program may use at most 128 MiB of HBM per device.

```python
import jax
import jax.numpy as jnp
from jax import lax

D = 5120
F = 20480
DWIN = 2560
FWIN = 10240
SEQ_GRP = 1
TENANTS = 2
SEQ_LEN = 256
TOKENS = 2048
SEQS = 8
N_GRP = 8


def draw_tenant(key, part):
    key = jax.random.fold_in(key, 7)
    order = jax.random.permutation(key, SEQS)
    return (order % TENANTS).astype(jnp.int32)


def block_levels(own_key, shape, split, low, largest):
    level, own = 1.0, jax.random.fold_in(own_key, 6)
    for position, blocks in split:
        steps = jnp.exp(jax.random.uniform(jax.random.fold_in(own, position), (blocks,), jnp.float32, low / len(split), largest / len(split)))
        level = level * jnp.repeat(steps, shape[position] // blocks).reshape([-1 if axis == position else 1 for axis in range(len(shape))])
    return level


def gaussian(key, shape, width, limit, shards=(), kind=jnp.bfloat16):
    gain = block_levels(key, shape, shards, -0.22, 0.18) if shards else 1.0
    drawn = jax.random.normal(key, shape, jnp.float32) * width * gain
    return jnp.minimum(jnp.maximum(drawn, -limit), limit).astype(kind)


def setup_inputs(seed: int = 0) -> dict:
    streams_of = jax.random.split(jax.random.key(seed), 6)
    return {
        "acts": gaussian(streams_of[0], (TOKENS, D), 1.0, 6.0, ((0, 256),)),
        "grads": gaussian(streams_of[1], (TOKENS, F), 1.0, 6.0, ((0, 256),)),
        "basis_in": gaussian(streams_of[2], (D, DWIN), D ** -0.5, 0.078125, ((1, 32),)),
        "basis_out": gaussian(streams_of[3], (F, FWIN), F ** -0.5, 0.0390625, ((0, 8), (1, 32))),
        "tenant": draw_tenant(jax.random.fold_in(streams_of[5], 71), 0),
    }


def reference(acts, grads, basis_in, basis_out, tenant):
    rotated_in = jnp.dot(acts, basis_in, preferred_element_type=jnp.float32).astype(jnp.bfloat16)
    rotated_out = jnp.dot(grads, basis_out, preferred_element_type=jnp.float32).astype(jnp.bfloat16)
    seq_count = SEQ_GRP * N_GRP
    rotated_in = rotated_in.reshape(seq_count, SEQ_LEN, DWIN)
    rotated_out = rotated_out.reshape(seq_count, SEQ_LEN, FWIN)
    owners = (tenant[:, None] == jnp.arange(TENANTS, dtype=jnp.int32)[None, :]).astype(jnp.float32)
    empty = jnp.zeros((TENANTS, FWIN, DWIN), jnp.float32)

    def per_group(accum, group):
        first = group * SEQ_GRP

        def per_sequence(inner, offset):
            index = (first + offset).astype(jnp.int32)
            left = lax.dynamic_index_in_dim(rotated_out, index, 0, keepdims=False)
            right = lax.dynamic_index_in_dim(rotated_in, index, 0, keepdims=False)
            corr = jnp.dot(left.T, right, preferred_element_type=jnp.float32)
            square = corr * corr
            weight = lax.dynamic_index_in_dim(owners, index, 0, keepdims=False)
            return inner + weight[:, None, None] * square[None], None

        partial_sum, unused = lax.scan(per_sequence, empty, jnp.arange(SEQ_GRP, dtype=jnp.int32))
        rounded = lax.optimization_barrier(partial_sum.astype(jnp.bfloat16)).astype(jnp.float32)
        return accum + rounded, None

    sums, unused = lax.scan(per_group, empty, jnp.arange(N_GRP, dtype=jnp.int32))
    total = jnp.sum(sums, axis=0)
    scale = 1.0 / float((seq_count - seq_count // TENANTS) * SEQ_LEN)
    return (total[None] - sums) * scale
```

```python
import jax
import jax.numpy as jnp
import numpy as np
from jax import lax
from jax.sharding import Mesh, PartitionSpec as P

SEQ_GRP = 1
TENANTS = 2
AXES = ("xl", "y", "xh", "z", "core")
SIZES = (2, 4, 2, 8, 2)
GRP = ("xl", "y")
PLANE = ("xl", "y", "xh")
BF16, F32 = jnp.bfloat16, jnp.float32


def shift(x, axis, step):
    count = SIZES[AXES.index(axis)]
    return lax.ppermute(x, axis, [(i, (i + step) % count) for i in range(count)])


def swapped(x, axis):
    other = shift(x, axis, 1)
    first = lax.axis_index(axis) == 0
    return jnp.stack([jnp.where(first, x, other), jnp.where(first, other, x)])


def shards(acts, grads, basis_in, basis_out, tenant):
    tokens, hidden = grads.shape
    model = acts.shape[1]
    own_in, own_out = basis_in.shape[1], basis_out.shape[1]
    groups, planes = 8, 16
    rows = hidden // planes

    sent = grads.reshape(tokens, planes, rows).transpose(1, 0, 2)
    panel = lax.all_to_all(sent, PLANE, 0, 0).reshape(planes * tokens, rows)

    halves = basis_out.T.reshape(own_out, 2, rows).transpose(1, 0, 2)
    mine = lax.all_to_all(halves, "xh", 0, 0)
    weights = jnp.stack([mine, shift(mine, "core", 1)], axis=1)
    weights = weights.reshape(2, 2 * own_out, rows)

    every = lax.all_gather(acts, "z", axis=0, tiled=True)
    pair = basis_in.T
    pair = swapped(pair, "xh")
    pair = swapped(pair, "core")
    cols = pair.transpose(1, 0, 2, 3).reshape(4 * own_in, model)
    rotated = lax.dot_general(
        cols, every, (((1,), (1,)), ((), ())), preferred_element_type=F32
    ).astype(BF16)
    blocks = lax.all_to_all(
        rotated.reshape(4, own_in, 8 * tokens), ("xh", "core"), 0, 0
    )
    blocks = blocks.transpose(1, 0, 2).reshape(own_in, 32 * tokens)
    spread = jnp.broadcast_to(blocks[None], (32,) + blocks.shape)
    rotated_in = lax.all_to_all(spread, ("xh", "z", "core"), 0, 0)
    rotated_in = rotated_in.reshape(32 * own_in, 32 * tokens)

    up, down = [panel], [panel]
    for _ in range(3):
        up.append(shift(up[-1], "z", 1))
        down.append(shift(down[-1], "z", -1))
    half = panel.shape[0] // 2
    last = jnp.concatenate(
        [shift(up[3][:half], "z", 1), shift(down[3][half:], "z", -1)], axis=0
    )

    def partial(parts):
        left = jnp.stack([p.reshape(groups, 2 * tokens, rows) for p in parts], axis=1)
        left = left.reshape(groups * len(parts) * 2 * tokens, rows)
        out = jnp.stack(
            [
                lax.dot_general(
                    left,
                    weights[h],
                    (((1,), (1,)), ((), ())),
                    preferred_element_type=F32,
                ).astype(BF16)
                for h in range(2)
            ]
        )
        out = out.reshape(planes, len(parts) * 2 * tokens, 2 * own_out)
        got = lax.all_to_all(out, ("xh", "xl", "y"), 0, 0)
        return jnp.sum(got.astype(F32), axis=0).astype(BF16)

    first = partial([panel, up[1], down[1], up[2], down[2]])
    second = partial([up[3], down[3], last])
    mixed = jnp.concatenate([first, second], axis=0)
    other = shift(mixed[:, own_out:], "core", 1)
    both = jnp.stack([mixed[:, :own_out], other]).reshape(2, 8, 2, tokens, own_out)

    core_rel, slot, half_x, row = np.unravel_index(
        np.arange(32 * tokens), (2, 8, 2, tokens)
    )
    offset = np.array([0, 7, 1, 6, 2, 5, 3, 4])[slot]
    core_of = (lax.axis_index("core") + core_rel) % 2
    z_of = (lax.axis_index("z") + offset) % 8
    source = ((half_x * 2 + core_of) * 8 + z_of) * tokens + row
    pick = (jnp.arange(32 * tokens)[:, None] == source[None, :]).astype(BF16)
    rolled = jnp.dot(
        rotated_in, pick, preferred_element_type=F32
    ).astype(BF16)

    left = both.reshape(32 * tokens, own_out)
    corr = lax.dot_general(
        left, rolled, (((0,), (1,)), ((), ())), preferred_element_type=F32
    )
    square = (corr * corr).astype(BF16)
    parts = lax.all_to_all(
        square.reshape(groups, own_out // groups, square.shape[1]), GRP, 0, 0
    ).astype(F32)
    sums = jnp.stack(
        [
            jnp.sum(jnp.where((tenant == k)[:, None, None], parts, 0.0), axis=0)
            for k in range(TENANTS)
        ]
    )
    total = jnp.sum(sums, axis=0)
    seq_count = SEQ_GRP * groups
    scale = 1.0 / float((seq_count - seq_count // TENANTS) * 32 * tokens)
    return (total[None] - sums) * scale


def solution(mesh):
    fine = Mesh(mesh.devices.reshape(SIZES), AXES)
    tile = ("xh", "z", "core")
    return jax.shard_map(
        shards,
        mesh=fine,
        in_specs=(
            P(AXES, None),
            P(AXES, None),
            P(None, tile),
            P(GRP, tile),
            P(),
        ),
        out_specs=P(None, tile + GRP, None),
        check_vma=False,
    )
```

```python
import jax
import jax.numpy as jnp
import numpy as np
from jax import lax
from jax.sharding import Mesh, PartitionSpec as P

SEQ_GRP = 1
TENANTS = 2
AXES = ("xl", "y", "xh", "z", "core")
SIZES = (2, 4, 2, 8, 2)
GRP = ("xl", "y")
PLANE = ("xl", "y", "xh")
BF16, F32 = jnp.bfloat16, jnp.float32
SLOTS = (0, 7, 1, 6, 2, 5, 3, 4)


def shift(x, axis, step):
    count = SIZES[AXES.index(axis)]
    return lax.ppermute(x, axis, [(i, (i + step) % count) for i in range(count)])


def after(x, *earlier):
    return lax.optimization_barrier((x,) + earlier)[0]


def ordered(x, other, axis):
    first = lax.axis_index(axis) == 0
    return jnp.stack([jnp.where(first, x, other), jnp.where(first, other, x)])


def rows_dot(a, b):
    return lax.dot_general(
        a, b, (((1,), (1,)), ((), ())), preferred_element_type=F32
    ).astype(BF16)


def shards(acts, grads, basis_in, basis_out, tenant):
    tokens, hidden = grads.shape
    model = acts.shape[1]
    own_in, own_out = basis_in.shape[1], basis_out.shape[1]
    groups, planes = 8, 16
    rows = hidden // planes
    xh, z = lax.axis_index("xh"), lax.axis_index("z")

    acts_x = shift(acts, "xh", 1)
    sent = grads.reshape(tokens, planes, rows).transpose(1, 0, 2)
    panel = lax.all_to_all(sent, PLANE, 0, 0).reshape(planes * tokens, rows)

    out_cols = basis_out.T
    keep = lax.dynamic_slice_in_dim(out_cols, xh * rows, rows, axis=1)
    give = lax.dynamic_slice_in_dim(out_cols, (1 - xh) * rows, rows, axis=1)

    pair = ordered(acts, acts_x, "xh").reshape(2 * tokens, model)
    give = after(give, panel)
    panel = after(panel, pair)
    every = lax.all_gather(pair, "z", axis=0, tiled=True)
    in_cols = basis_in.T
    in_other = shift(in_cols, "core", 1)

    keep_c = shift(keep, "core", 1)
    got = shift(give, "xh", 1)

    def partial(parts):
        left = jnp.stack([p.reshape(groups, 2 * tokens, rows) for p in parts], axis=1)
        left = left.reshape(groups * len(parts) * 2 * tokens, rows)
        out = jnp.stack([rows_dot(left, weights[h]) for h in range(2)])
        return out.reshape(planes, len(parts) * 2 * tokens, 2 * own_out)

    def home(out):
        back = lax.all_to_all(out, ("xh", "xl", "y"), 0, 0)
        return jnp.sum(back.astype(F32), axis=0).astype(BF16)

    up, down = [panel], [panel]
    for _ in range(2):
        up.append(shift(up[-1], "z", 1))
        down.append(shift(down[-1], "z", -1))
    got = after(got, up[1], down[1])
    got_c = shift(got, "core", 1)
    weights = ordered(
        jnp.concatenate([keep, keep_c]), jnp.concatenate([got, got_c]), "xh"
    )
    out_first = partial([panel, up[1], down[1], up[2], down[2]])
    up.append(shift(after(up[2], out_first), "z", 1))
    down.append(shift(after(down[2], out_first), "z", -1))
    half = panel.shape[0] // 2
    last = jnp.concatenate(
        [shift(up[3][:half], "z", 1), shift(down[3][half:], "z", -1)], axis=0
    )
    first = home(out_first)

    r = rows_dot(jnp.concatenate([in_cols, in_other]), every)
    r = r.reshape(2, own_in, 16 * tokens)
    r = jnp.where(lax.axis_index("core") == 0, r, r[::-1])
    r = r.reshape(2 * own_in, 16 * tokens)
    far = shift(r, "z", 4)
    duo = jnp.stack([r, far])
    below, above, two = shift(duo, "z", 1), shift(duo, "z", -1), shift(duo, "z", 2)
    ring = [r, above[0], two[1], below[1], far, above[1], two[0], below[0]]
    r = lax.dynamic_slice_in_dim(jnp.stack(ring + ring[:7]), (8 - z) % 8, 8, axis=0)
    r = r.reshape(16 * own_in, 16 * tokens)
    slot, half_x, row = np.unravel_index(np.arange(16 * tokens), (8, 2, tokens))
    z_of = (z + np.array(SLOTS)[slot]) % 8
    source = (z_of * 2 + half_x) * tokens + row
    pick = (jnp.arange(16 * tokens)[:, None] == source[None, :]).astype(BF16)
    r = jnp.dot(r, pick, preferred_element_type=F32).astype(BF16)
    r = ordered(r, shift(r, "xh", 1), "xh").reshape(32 * own_in, 16 * tokens)
    rotated_in = jnp.concatenate([r, shift(r, "core", 1)], axis=1)

    second = home(after(partial([up[3], down[3], last]), first))
    mixed = jnp.concatenate([first, second], axis=0)
    other = shift(mixed[:, own_out:], "core", 1)
    left = jnp.concatenate([mixed[:, :own_out], other], axis=0)

    corr = lax.dot_general(
        left, rotated_in, (((0,), (1,)), ((), ())), preferred_element_type=F32
    )
    square = (corr * corr).astype(BF16)
    parts = lax.all_to_all(
        square.reshape(groups, own_out // groups, square.shape[1]), GRP, 0, 0
    ).astype(F32)
    sums = jnp.stack(
        [
            jnp.sum(jnp.where((tenant == k)[:, None, None], parts, 0.0), axis=0)
            for k in range(TENANTS)
        ]
    )
    total = jnp.sum(sums, axis=0)
    seq_count = SEQ_GRP * groups
    scale = 1.0 / float((seq_count - seq_count // TENANTS) * 32 * tokens)
    return (total[None] - sums) * scale


def solution(mesh):
    fine = Mesh(mesh.devices.reshape(SIZES), AXES)
    tile = ("xh", "z", "core")
    return jax.shard_map(
        shards,
        mesh=fine,
        in_specs=(
            P(AXES, None),
            P(AXES, None),
            P(None, tile),
            P(GRP, tile),
            P(),
        ),
        out_specs=P(None, tile + GRP, None),
        check_vma=False,
    )
```

```python
import jax
import jax.numpy as jnp
import numpy as np
from jax import lax
from jax.experimental import pallas as pl
from jax.experimental.pallas import tpu as pltpu
from jax.sharding import Mesh, PartitionSpec as P

SEQ_GRP = 1
TENANTS = 2
AXES = ("xl", "y", "xh", "z", "core")
SIZES = (2, 4, 2, 8, 2)
GRP = ("xl", "y")
BF16, F32 = jnp.bfloat16, jnp.float32


def shift(x, axis, step=1):
    count = SIZES[AXES.index(axis)]
    return lax.ppermute(x, axis, [(i, (i + step) % count) for i in range(count)])


def stage(*arrays):
    return lax.optimization_barrier(arrays)


def ordered(x, other, axis):
    first = lax.axis_index(axis) == 0
    return jnp.concatenate([jnp.where(first, x, other), jnp.where(first, other, x)])


def rows_dot(a, b):
    return lax.dot_general(
        a, b, (((1,), (1,)), ((), ())), preferred_element_type=F32
    ).astype(BF16)


def product_kernel(spans, xh_ref, *refs):
    out_ref, left, right, sems = refs[-4:]
    sources, pieces = refs[: len(spans)], refs[len(spans) : -4]
    copies, row = [], 0
    for k, (ref, (first, rows)) in enumerate(zip(sources, spans)):
        copies.append(
            pltpu.make_async_copy(
                ref.at[pl.ds(first, rows)], left.at[pl.ds(row, rows)], sems.at[k]
            )
        )
        row += rows
    row = 0
    for k, ref in enumerate(pieces, len(spans)):
        place = right.at[pl.ds(row, ref.shape[0])]
        copies.append(pltpu.make_async_copy(ref, place, sems.at[k]))
        row += ref.shape[0]
    for copy in copies:
        copy.start()
    groups, cols = out_ref.shape[1], out_ref.shape[3]
    step = 16
    waited = 0
    for half, ready in enumerate((len(spans) + 2, len(copies))):
        for copy in copies[waited:ready]:
            copy.wait()
        waited = ready
        out = lax.dot_general(
            left[...],
            right[half * cols : (half + 1) * cols],
            (((1,), (1,)), ((), ())),
            preferred_element_type=F32,
        ).astype(BF16)
        side = (xh_ref[0] + half) % 2
        for slot in range(left.shape[0] // (groups * step)):
            for group in range(groups):
                row = (slot * groups + group) * step
                out_ref[side, group, slot * step : (slot + 1) * step] = out[
                    row : row + step
                ]


def product(parts, pieces, xh):
    arrays = [p[0] for p in parts]
    depth = arrays[0].shape[1]
    total = sum(p[2] for p in parts)
    cols = sum(p.shape[0] for p in pieces)
    spans = [p[1:] for p in parts]
    return pl.pallas_call(
        lambda *refs: product_kernel(spans, *refs),
        out_shape=jax.ShapeDtypeStruct((2, 8, total // 8, cols // 2), BF16),
        in_specs=[pl.BlockSpec(memory_space=pltpu.SMEM)]
        + [pl.BlockSpec(memory_space=pl.ANY)] * (len(parts) + len(pieces)),
        out_specs=pl.BlockSpec(memory_space=pltpu.VMEM),
        scratch_shapes=[
            pltpu.VMEM((total, depth), BF16),
            pltpu.VMEM((cols, depth), BF16),
            pltpu.SemaphoreType.DMA((len(parts) + len(pieces),)),
        ],
        compiler_params=pltpu.CompilerParams(vmem_limit_bytes=40 << 20),
        cost_estimate=pl.CostEstimate(
            flops=2 * total * depth * cols,
            bytes_accessed=2 * (total * depth + cols * depth + total * cols),
            transcendentals=0,
        ),
    )(xh.reshape(1).astype(jnp.int32), *arrays, *pieces)


def inputs_kernel(spans, core_ref, *refs):
    own, other, out_ref, chunks, sems = refs[-5:]
    copies = []
    for k, (ref, (first, rows)) in enumerate(zip(refs[: len(spans)], spans)):
        source = ref.at[pl.ds(first, rows)]
        copies.append(pltpu.make_async_copy(source, chunks.at[k], sems.at[k]))
    for copy in copies:
        copy.start()
    for copy in copies:
        copy.wait()
    wide = [chunks[k].astype(F32) for k in range(len(spans))]
    depth = chunks.shape[2]
    quarters = own.shape[1] // depth
    totals = [0.0, 0.0]
    for q in range(quarters):
        rows = [
            w[first : first + 8]
            for w in wide
            for first in (q * 8, (quarters + q) * 8)
        ]
        heard = jnp.concatenate(rows).astype(BF16)
        for side, cols in enumerate((own, other)):
            totals[side] += lax.dot_general(
                cols[:, q * depth : (q + 1) * depth],
                heard,
                (((1,), (1,)), ((), ())),
                preferred_element_type=F32,
            )
    for side in range(2):
        out_ref[(core_ref[0] + side) % 2] = totals[side].astype(BF16)


def inputs(parts, own, other, core):
    arrays = [p[0] for p in parts]
    spans = [p[1:] for p in parts]
    rows, depth = spans[0][1], arrays[0].shape[1]
    tokens = rows * depth // own.shape[1] * len(parts)
    return pl.pallas_call(
        lambda *refs: inputs_kernel(spans, *refs),
        out_shape=jax.ShapeDtypeStruct((2, own.shape[0], tokens), BF16),
        in_specs=[pl.BlockSpec(memory_space=pltpu.SMEM)]
        + [pl.BlockSpec(memory_space=pl.ANY)] * len(parts)
        + [pl.BlockSpec(memory_space=pltpu.VMEM)] * 2,
        out_specs=pl.BlockSpec(memory_space=pltpu.VMEM),
        scratch_shapes=[
            pltpu.VMEM((len(parts), rows, depth), BF16),
            pltpu.SemaphoreType.DMA((len(parts),)),
        ],
        compiler_params=pltpu.CompilerParams(vmem_limit_bytes=24 << 20),
        cost_estimate=pl.CostEstimate(
            flops=4 * own.size * tokens,
            bytes_accessed=4 * own.size + 2 * len(parts) * rows * depth,
            transcendentals=0,
        ),
    )(core.reshape(1).astype(jnp.int32), *arrays, own, other)


def arrange_kernel(place_ref, near, below, above, two, out_ref):
    xh, z = place_ref[0], place_ref[1]
    for steps, ref, far in (
        (0, near, 0),
        (1, above, 0),
        (2, two, 1),
        (3, below, 1),
        (4, near, 1),
        (5, above, 1),
        (6, two, 0),
        (7, below, 0),
    ):
        for side in range(2):
            out_ref[(xh + side) % 2, (z + steps) % 8] = ref[far, side]


def arrange(place, *pieces):
    return pl.pallas_call(
        arrange_kernel,
        out_shape=jax.ShapeDtypeStruct((2, 8) + pieces[0].shape[2:], BF16),
        in_specs=[pl.BlockSpec(memory_space=pltpu.SMEM)]
        + [pl.BlockSpec(memory_space=pltpu.VMEM)] * 4,
        out_specs=pl.BlockSpec(memory_space=pltpu.VMEM),
        compiler_params=pltpu.CompilerParams(vmem_limit_bytes=16 << 20),
    )(place, *pieces)


def shards(acts, grads, basis_in, basis_out, tenant):
    tokens, hidden = grads.shape
    model = acts.shape[1]
    own_in, own_out = basis_in.shape[1], basis_out.shape[1]
    groups, planes = 8, 16
    rows = hidden // planes
    xh, z, core = (lax.axis_index(a) for a in ("xh", "z", "core"))

    in_cols = basis_in.T
    in_other = shift(in_cols, "core")
    acts_x = shift(acts, "xh")
    step = lambda i: ((i // 2 + 1 - 2 * (i % 2)) % 8) * 2 + i % 2
    turn = [(i, step(i)) for i in range(16)]
    over = [(i, step(i ^ 1)) for i in range(16)]
    ring = lambda x, way=turn: lax.ppermute(x, ("z", "core"), way)
    quarters = model // rows
    tall = lambda a: a.reshape(tokens, quarters, rows).transpose(1, 0, 2).reshape(-1, rows)
    own_acts = jnp.concatenate([tall(acts), tall(acts_x)])
    acts_1 = [ring(own_acts), ring(own_acts, over)]

    sent = grads.reshape(tokens, planes, rows).transpose(1, 0, 2)
    panel = lax.all_to_all(sent, ("xl", "y", "xh"), 0, 0).reshape(planes * tokens, rows)

    out_cols = basis_out.T
    keep = lax.dynamic_slice_in_dim(out_cols, xh * rows, rows, axis=1)
    give = lax.dynamic_slice_in_dim(out_cols, (1 - xh) * rows, rows, axis=1)
    panel, keep, give, *acts_1 = stage(panel, keep, give, *acts_1)
    size, extra = panel.shape[0], own_acts.shape[0]
    keep_c = shift(keep, "core")
    turned = ring(jnp.concatenate([panel, *acts_1]))
    crossed = ring(panel, over)
    got = [shift(give[: own_out // 2], "xh")]
    give, got[0], turned, crossed = stage(give, got[0], turned, crossed)
    block_2 = ring(jnp.concatenate([turned[:size], crossed, turned[size:]]))
    got.append(shift(give[own_out // 2 :], "xh"))
    got[1], block_2 = stage(got[1], block_2)
    got_c = shift(jnp.concatenate(got), "core")
    block_3 = ring(block_2[: 2 * size + extra])
    pieces = (keep, keep_c, *got, got_c)
    parts = [(panel, 0), (turned, 0), (crossed, 0), (block_2, 0), (block_2, size)]
    out = product([(*p, size) for p in parts], pieces, xh)
    out, block_3, in_cols, in_other, *pieces = stage(
        out, block_3, in_cols, in_other, *pieces
    )

    def home(out):
        out = out.reshape(planes, out.shape[2], 2 * own_out)
        return lax.all_to_all(out, ("xh", "xl", "y"), 0, 0)

    first = home(out)
    last = ring(block_3[:size])

    parts = [
        (own_acts, 0),
        *((a, 0) for a in acts_1),
        *((turned, size + k * extra) for k in range(2)),
        *((block_2, 2 * size + k * extra) for k in range(2)),
        (block_3, 2 * size),
    ]
    r = inputs([(*p, extra) for p in parts], in_cols, in_other, core).reshape(2 * own_in, 16 * tokens)
    r = jnp.concatenate([r, shift(r, "core")], axis=1)
    z_j, xh_j, row = np.unravel_index(np.arange(16 * tokens), (8, 2, tokens))
    apart = (z_j - z) % 8
    ran = jnp.where(apart % 4 == 0, core, (apart < 4).astype(core.dtype))
    away = jnp.minimum(apart, 8 - apart)
    slot = jnp.where(away == 0, 0, jnp.where(away == 4, 7, 2 * away - 1 + (ran ^ core)))
    source = (((ran ^ core) * 8 + slot) * 2 + (xh_j ^ xh)) * tokens + row
    pick = (jnp.arange(32 * tokens)[:, None] == source[None, :]).astype(BF16)
    r = jnp.dot(r, pick, preferred_element_type=F32).astype(BF16)

    far = shift(r, "z", 4)
    cross = shift(r, "xh")
    both = [((a, b), (1 - a, (b + 4) % 8)) for a in range(2) for b in range(8)]
    far_cross = lax.ppermute(
        r, ("xh", "z"), [(a * 8 + b, c * 8 + d) for (a, b), (c, d) in both]
    )
    parts = [(block_3, 0, size), (block_3, size, size), (last, 0, size)]
    out = product(parts, pieces, xh)
    out, first, r, far, cross, far_cross = stage(out, first, r, far, cross, far_cross)
    second = home(out)

    quad = jnp.stack([jnp.stack([r, cross]), jnp.stack([far, far_cross])])
    below, above, two = shift(quad, "z", 1), shift(quad, "z", -1), shift(quad, "z", 2)
    place = jnp.stack([xh, z]).astype(jnp.int32)
    r = arrange(place, quad, below, above, two).reshape(32 * own_in, 16 * tokens)
    r = jnp.concatenate([r, shift(r, "core")], axis=1)
    side, slot, half_x, row = np.unravel_index(
        np.arange(32 * tokens), (2, 8, 2, tokens)
    )
    ran = core ^ side
    steps = np.array([0, 1, 1, 2, 2, 3, 3, 4])[slot]
    from_core = ran ^ np.where(np.isin(slot, (0, 7)), 0, (slot - 1) % 2)
    z_of = (z + (2 * ran - 1) * steps) % 8
    source = (((from_core ^ core) * 8 + z_of) * 2 + half_x) * tokens + row
    pick = (jnp.arange(32 * tokens)[:, None] == source[None, :]).astype(BF16)
    rotated_in = jnp.dot(r, pick, preferred_element_type=F32).astype(BF16)

    mixed = jnp.concatenate(
        [jnp.sum(p.astype(F32), axis=0).astype(BF16) for p in (first, second)]
    )
    left = jnp.concatenate([mixed[:, :own_out], shift(mixed[:, own_out:], "core")])

    corr = lax.dot_general(
        left, rotated_in, (((0,), (1,)), ((), ())), preferred_element_type=F32
    )
    square = (corr * corr).astype(BF16)
    parts = lax.all_to_all(
        square.reshape(groups, own_out // groups, square.shape[1]), GRP, 0, 0
    ).astype(F32)
    sums = jnp.stack(
        [
            jnp.sum(jnp.where((tenant == k)[:, None, None], parts, 0.0), axis=0)
            for k in range(TENANTS)
        ]
    )
    total = jnp.sum(sums, axis=0)
    seq_count = SEQ_GRP * groups
    scale = 1.0 / float((seq_count - seq_count // TENANTS) * 32 * tokens)
    return (total[None] - sums) * scale


def solution(mesh):
    fine = Mesh(mesh.devices.reshape(SIZES), AXES)
    tile = ("xh", "z", "core")
    return jax.shard_map(
        shards,
        mesh=fine,
        in_specs=(
            P(AXES, None),
            P(AXES, None),
            P(None, tile),
            P(GRP, tile),
            P(),
        ),
        out_specs=P(None, tile + GRP, None),
        check_vma=False,
    )
```

```python
import jax
import jax.numpy as jnp
import numpy as np
from jax import lax
from jax.experimental import pallas as pl
from jax.experimental.pallas import tpu as pltpu
from jax.sharding import Mesh, PartitionSpec as P

SEQ_GRP = 1
TENANTS = 2
AXES = ("xl", "y", "xh", "z", "core")
SIZES = (2, 4, 2, 8, 2)
GRP = ("xl", "y")
BF16, F32 = jnp.bfloat16, jnp.float32


def shift(x, axis, step=1):
    count = SIZES[AXES.index(axis)]
    return lax.ppermute(x, axis, [(i, (i + step) % count) for i in range(count)])


def stage(*arrays):
    return lax.optimization_barrier(arrays)


def ordered(x, other, axis):
    first = lax.axis_index(axis) == 0
    return jnp.concatenate([jnp.where(first, x, other), jnp.where(first, other, x)])


def rows_dot(a, b):
    return lax.dot_general(
        a, b, (((1,), (1,)), ((), ())), preferred_element_type=F32
    ).astype(BF16)


def product_kernel(spans, xh_ref, *refs):
    out_ref, left, right, ready_out, sems = refs[-5:]
    sources, pieces = refs[: len(spans)], refs[len(spans) : -5]
    copies, row = [], 0
    for k, (ref, (first, rows)) in enumerate(zip(sources, spans)):
        copies.append(
            pltpu.make_async_copy(
                ref.at[pl.ds(first, rows)], left.at[pl.ds(row, rows)], sems.at[k]
            )
        )
        row += rows
    row = 0
    for k, ref in enumerate(pieces, len(spans)):
        place = right.at[pl.ds(row, ref.shape[0])]
        copies.append(pltpu.make_async_copy(ref, place, sems.at[k]))
        row += ref.shape[0]
    for copy in copies:
        copy.start()
    groups, cols = out_ref.shape[1], out_ref.shape[3]
    step = 16
    waited, sent = 0, []
    for half, ready in enumerate((len(spans) + 2, len(copies))):
        for copy in copies[waited:ready]:
            copy.wait()
        waited = ready
        out = lax.dot_general(
            left[...],
            right[half * cols : (half + 1) * cols],
            (((1,), (1,)), ((), ())),
            preferred_element_type=F32,
        ).astype(BF16)
        side = (xh_ref[0] + half) % 2
        for slot in range(left.shape[0] // (groups * step)):
            for group in range(groups):
                row = (slot * groups + group) * step
                ready_out[half, group, slot * step : (slot + 1) * step] = out[
                    row : row + step
                ]
        send = pltpu.make_async_copy(
            ready_out.at[half], out_ref.at[side], sems.at[len(copies) + half]
        )
        send.start()
        sent.append(send)
    for send in sent:
        send.wait()


def product(parts, pieces, xh):
    arrays = [p[0] for p in parts]
    depth = arrays[0].shape[1]
    total = sum(p[2] for p in parts)
    cols = sum(p.shape[0] for p in pieces)
    spans = [p[1:] for p in parts]
    return pl.pallas_call(
        lambda *refs: product_kernel(spans, *refs),
        out_shape=jax.ShapeDtypeStruct((2, 8, total // 8, cols // 2), BF16),
        in_specs=[pl.BlockSpec(memory_space=pltpu.SMEM)]
        + [pl.BlockSpec(memory_space=pl.ANY)] * (len(parts) + len(pieces)),
        out_specs=pl.BlockSpec(memory_space=pltpu.HBM),
        scratch_shapes=[
            pltpu.VMEM((total, depth), BF16),
            pltpu.VMEM((cols, depth), BF16),
            pltpu.VMEM((2, 8, total // 8, cols // 2), BF16),
            pltpu.SemaphoreType.DMA((len(parts) + len(pieces) + 2,)),
        ],
        compiler_params=pltpu.CompilerParams(vmem_limit_bytes=40 << 20),
        cost_estimate=pl.CostEstimate(
            flops=2 * total * depth * cols,
            bytes_accessed=2 * (total * depth + cols * depth + total * cols),
            transcendentals=0,
        ),
    )(xh.reshape(1).astype(jnp.int32), *arrays, *pieces)


def inputs_kernel(spans, core_ref, *refs):
    out_ref, chunks, wide_cols, sems = refs[-4:]
    copies = [
        pltpu.make_async_copy(ref, wide_cols.at[k], sems.at[len(spans) + k])
        for k, ref in enumerate(refs[len(spans) : len(spans) + 2])
    ]
    for k, (ref, (first, rows)) in enumerate(zip(refs[: len(spans)], spans)):
        source = ref.at[pl.ds(first, rows)]
        copies.append(pltpu.make_async_copy(source, chunks.at[k], sems.at[k]))
    for copy in copies:
        copy.start()
    for copy in copies:
        copy.wait()
    wide = [chunks[k].astype(F32) for k in range(len(spans))]
    depth = chunks.shape[2]
    quarters = wide_cols.shape[2] // depth
    totals = [0.0, 0.0]
    for q in range(quarters):
        rows = [
            w[first : first + 8]
            for w in wide
            for first in (q * 8, (quarters + q) * 8)
        ]
        heard = jnp.concatenate(rows).astype(BF16)
        for side in range(2):
            totals[side] += lax.dot_general(
                wide_cols[side, :, q * depth : (q + 1) * depth],
                heard,
                (((1,), (1,)), ((), ())),
                preferred_element_type=F32,
            )
    for side in range(2):
        out_ref[(core_ref[0] + side) % 2] = totals[side].astype(BF16)


def inputs(parts, own, other, core):
    arrays = [p[0] for p in parts]
    spans = [p[1:] for p in parts]
    rows, depth = spans[0][1], arrays[0].shape[1]
    tokens = rows * depth // own.shape[1] * len(parts)
    return pl.pallas_call(
        lambda *refs: inputs_kernel(spans, *refs),
        out_shape=jax.ShapeDtypeStruct((2, own.shape[0], tokens), BF16),
        in_specs=[pl.BlockSpec(memory_space=pltpu.SMEM)]
        + [pl.BlockSpec(memory_space=pltpu.HBM)] * (len(parts) + 2),
        out_specs=pl.BlockSpec(memory_space=pltpu.VMEM),
        scratch_shapes=[
            pltpu.VMEM((len(parts), rows, depth), BF16),
            pltpu.VMEM((2,) + own.shape, BF16),
            pltpu.SemaphoreType.DMA((len(parts) + 2,)),
        ],
        compiler_params=pltpu.CompilerParams(vmem_limit_bytes=60 << 20),
        cost_estimate=pl.CostEstimate(
            flops=4 * own.size * tokens,
            bytes_accessed=4 * own.size + 2 * len(parts) * rows * depth,
            transcendentals=0,
        ),
    )(core.reshape(1).astype(jnp.int32), *arrays, own, other)


def arrange_kernel(place_ref, near, below, above, two, out_ref):
    xh, z = place_ref[0], place_ref[1]
    for steps, ref, far in (
        (0, near, 0),
        (1, above, 0),
        (2, two, 1),
        (3, below, 1),
        (4, near, 1),
        (5, above, 1),
        (6, two, 0),
        (7, below, 0),
    ):
        for side in range(2):
            out_ref[(xh + side) % 2, (z + steps) % 8] = ref[far, side]


def arrange(place, *pieces):
    return pl.pallas_call(
        arrange_kernel,
        out_shape=jax.ShapeDtypeStruct((2, 8) + pieces[0].shape[2:], BF16),
        in_specs=[pl.BlockSpec(memory_space=pltpu.SMEM)]
        + [pl.BlockSpec(memory_space=pltpu.VMEM)] * 4,
        out_specs=pl.BlockSpec(memory_space=pltpu.VMEM),
        compiler_params=pltpu.CompilerParams(vmem_limit_bytes=16 << 20),
    )(place, *pieces)


def shards(acts, grads, basis_in, basis_out, tenant):
    tokens, hidden = grads.shape
    model = acts.shape[1]
    own_in, own_out = basis_in.shape[1], basis_out.shape[1]
    groups, planes = 8, 16
    rows = hidden // planes
    xh, z, core = (lax.axis_index(a) for a in ("xh", "z", "core"))

    in_cols = basis_in.T
    in_other = shift(in_cols, "core")
    acts_x = shift(acts, "xh")
    step = lambda i: ((i // 2 + 1 - 2 * (i % 2)) % 8) * 2 + i % 2
    turn = [(i, step(i)) for i in range(16)]
    over = [(i, step(i ^ 1)) for i in range(16)]
    ring = lambda x, way=turn: lax.ppermute(x, ("z", "core"), way)
    quarters = model // rows
    tall = lambda a: a.reshape(tokens, quarters, rows).transpose(1, 0, 2).reshape(-1, rows)
    own_acts = jnp.concatenate([tall(acts), tall(acts_x)])
    acts_1 = [ring(own_acts), ring(own_acts, over)]

    sent = grads.reshape(tokens, planes, rows).transpose(1, 0, 2)
    panel = lax.all_to_all(sent, ("xl", "y", "xh"), 0, 0).reshape(planes * tokens, rows)

    out_cols = basis_out.T
    keep = lax.dynamic_slice_in_dim(out_cols, xh * rows, rows, axis=1)
    give = lax.dynamic_slice_in_dim(out_cols, (1 - xh) * rows, rows, axis=1)
    panel, keep, give, *acts_1 = stage(panel, keep, give, *acts_1)
    size, extra = panel.shape[0], own_acts.shape[0]
    keep_c = shift(keep, "core")
    turned = ring(jnp.concatenate([panel, *acts_1]))
    crossed = ring(panel, over)
    got = [shift(give[: own_out // 2], "xh")]
    give, got[0], turned, crossed = stage(give, got[0], turned, crossed)
    block_2 = ring(jnp.concatenate([turned[:size], crossed, turned[size:]]))
    got.append(shift(give[own_out // 2 :], "xh"))
    got_c = [shift(got[0], "core")]
    got[1], block_2 = stage(got[1], block_2)
    got_c.append(shift(got[1], "core"))
    block_3 = ring(block_2[: 2 * size + extra])
    pieces = (keep, keep_c, *got, *got_c)
    parts = [(panel, 0), (turned, 0), (crossed, 0), (block_2, 0), (block_2, size)]
    out = product([(*p, size) for p in parts], pieces, xh)
    out, block_3, in_cols, in_other, *pieces = stage(
        out, block_3, in_cols, in_other, *pieces
    )

    def home(out):
        out = out.reshape(planes, out.shape[2], 2 * own_out)
        return lax.all_to_all(out, ("xh", "xl", "y"), 0, 0)

    first = home(out)
    last = ring(block_3[:size])

    parts = [
        (own_acts, 0),
        *((a, 0) for a in acts_1),
        *((turned, size + k * extra) for k in range(2)),
        *((block_2, 2 * size + k * extra) for k in range(2)),
        (block_3, 2 * size),
    ]
    r = inputs([(*p, extra) for p in parts], in_cols, in_other, core).reshape(2 * own_in, 16 * tokens)
    r = jnp.concatenate([r, shift(r, "core")], axis=1)
    z_j, xh_j, row = np.unravel_index(np.arange(16 * tokens), (8, 2, tokens))
    apart = (z_j - z) % 8
    ran = jnp.where(apart % 4 == 0, core, (apart < 4).astype(core.dtype))
    away = jnp.minimum(apart, 8 - apart)
    slot = jnp.where(away == 0, 0, jnp.where(away == 4, 7, 2 * away - 1 + (ran ^ core)))
    source = (((ran ^ core) * 8 + slot) * 2 + (xh_j ^ xh)) * tokens + row
    pick = (jnp.arange(32 * tokens)[:, None] == source[None, :]).astype(BF16)
    r = jnp.dot(r, pick, preferred_element_type=F32).astype(BF16)

    far = shift(r, "z", 4)
    cross = shift(r, "xh")
    both = [((a, b), (1 - a, (b + 4) % 8)) for a in range(2) for b in range(8)]
    far_cross = lax.ppermute(
        r, ("xh", "z"), [(a * 8 + b, c * 8 + d) for (a, b), (c, d) in both]
    )
    parts = [(block_3, 0, size), (block_3, size, size), (last, 0, size)]
    out = product(parts, pieces, xh)
    out, first, r, far, cross, far_cross = stage(out, first, r, far, cross, far_cross)
    second = home(out)

    quad = jnp.stack([jnp.stack([r, cross]), jnp.stack([far, far_cross])])
    below, above, two = shift(quad, "z", 1), shift(quad, "z", -1), shift(quad, "z", 2)
    place = jnp.stack([xh, z]).astype(jnp.int32)
    r = arrange(place, quad, below, above, two).reshape(32 * own_in, 16 * tokens)
    r = jnp.concatenate([r, shift(r, "core")], axis=1)
    side, slot, half_x, row = np.unravel_index(
        np.arange(32 * tokens), (2, 8, 2, tokens)
    )
    ran = core ^ side
    steps = np.array([0, 1, 1, 2, 2, 3, 3, 4])[slot]
    from_core = ran ^ np.where(np.isin(slot, (0, 7)), 0, (slot - 1) % 2)
    z_of = (z + (2 * ran - 1) * steps) % 8
    source = (((from_core ^ core) * 8 + z_of) * 2 + half_x) * tokens + row
    pick = (jnp.arange(32 * tokens)[:, None] == source[None, :]).astype(BF16)
    rotated_in = jnp.dot(r, pick, preferred_element_type=F32).astype(BF16)

    mixed = jnp.concatenate(
        [jnp.sum(p.astype(F32), axis=0).astype(BF16) for p in (first, second)]
    )
    left = jnp.concatenate([mixed[:, :own_out], shift(mixed[:, own_out:], "core")])

    corr = lax.dot_general(
        left, rotated_in, (((0,), (1,)), ((), ())), preferred_element_type=F32
    )
    square = (corr * corr).astype(BF16)
    parts = lax.all_to_all(
        square.reshape(groups, own_out // groups, square.shape[1]), GRP, 0, 0
    ).astype(F32)
    sums = jnp.stack(
        [
            jnp.sum(jnp.where((tenant == k)[:, None, None], parts, 0.0), axis=0)
            for k in range(TENANTS)
        ]
    )
    total = jnp.sum(sums, axis=0)
    seq_count = SEQ_GRP * groups
    scale = 1.0 / float((seq_count - seq_count // TENANTS) * 32 * tokens)
    return (total[None] - sums) * scale


def solution(mesh):
    fine = Mesh(mesh.devices.reshape(SIZES), AXES)
    tile = ("xh", "z", "core")
    return jax.shard_map(
        shards,
        mesh=fine,
        in_specs=(
            P(AXES, None),
            P(AXES, None),
            P(None, tile),
            P(GRP, tile),
            P(),
        ),
        out_specs=P(None, tile + GRP, None),
        check_vma=False,
    )
```

```python
import jax
import jax.numpy as jnp
import numpy as np
from jax import lax
from jax.experimental import pallas as pl
from jax.experimental.pallas import tpu as pltpu
from jax.sharding import Mesh, PartitionSpec as P

SEQ_GRP = 1
TENANTS = 2
AXES = ("xl", "y", "xh", "z", "core")
SIZES = (2, 4, 2, 8, 2)
GRP = ("xl", "y")
BF16, F32 = jnp.bfloat16, jnp.float32


def shift(x, axis, step=1):
    count = SIZES[AXES.index(axis)]
    return lax.ppermute(x, axis, [(i, (i + step) % count) for i in range(count)])


def stage(*arrays):
    return lax.optimization_barrier(arrays)


def ordered(x, other, axis):
    first = lax.axis_index(axis) == 0
    return jnp.concatenate([jnp.where(first, x, other), jnp.where(first, other, x)])


def rows_dot(a, b):
    return lax.dot_general(
        a, b, (((1,), (1,)), ((), ())), preferred_element_type=F32
    ).astype(BF16)


def product_kernel(spans, xh_ref, *refs):
    out_ref, left, right, ready_out, sems = refs[-5:]
    sources, pieces = refs[: len(spans)], refs[len(spans) : -5]
    copies, row = [], 0
    for k, (ref, (first, rows)) in enumerate(zip(sources, spans)):
        copies.append(
            pltpu.make_async_copy(
                ref.at[pl.ds(first, rows)], left.at[pl.ds(row, rows)], sems.at[k]
            )
        )
        row += rows
    row = 0
    for k, ref in enumerate(pieces, len(spans)):
        place = right.at[pl.ds(row, ref.shape[0])]
        copies.append(pltpu.make_async_copy(ref, place, sems.at[k]))
        row += ref.shape[0]
    for copy in copies:
        copy.start()
    groups, cols = out_ref.shape[1], out_ref.shape[3]
    step = 16
    waited, sent = 0, []
    for half, ready in enumerate((len(spans) + 2, len(copies))):
        for copy in copies[waited:ready]:
            copy.wait()
        waited = ready
        out = lax.dot_general(
            left[...],
            right[half * cols : (half + 1) * cols],
            (((1,), (1,)), ((), ())),
            preferred_element_type=F32,
        ).astype(BF16)
        side = (xh_ref[0] + half) % 2
        for slot in range(left.shape[0] // (groups * step)):
            for group in range(groups):
                row = (slot * groups + group) * step
                ready_out[half, group, slot * step : (slot + 1) * step] = out[
                    row : row + step
                ]
        send = pltpu.make_async_copy(
            ready_out.at[half], out_ref.at[side], sems.at[len(copies) + half]
        )
        send.start()
        sent.append(send)
    for send in sent:
        send.wait()


def product(parts, pieces, xh, grant):
    arrays = [p[0] for p in parts]
    depth = arrays[0].shape[1]
    total = sum(p[2] for p in parts)
    cols = sum(p.shape[0] for p in pieces)
    spans = [p[1:] for p in parts]
    return pl.pallas_call(
        lambda *refs: product_kernel(spans, *refs),
        out_shape=jax.ShapeDtypeStruct((2, 8, total // 8, cols // 2), BF16),
        in_specs=[pl.BlockSpec(memory_space=pltpu.SMEM)]
        + [pl.BlockSpec(memory_space=pl.ANY)] * (len(parts) + len(pieces)),
        out_specs=pl.BlockSpec(memory_space=pltpu.HBM),
        scratch_shapes=[
            pltpu.VMEM((total, depth), BF16),
            pltpu.VMEM((cols, depth), BF16),
            pltpu.VMEM((2, 8, total // 8, cols // 2), BF16),
            pltpu.SemaphoreType.DMA((len(parts) + len(pieces) + 2,)),
        ],
        compiler_params=pltpu.CompilerParams(vmem_limit_bytes=grant << 20),
        cost_estimate=pl.CostEstimate(
            flops=2 * total * depth * cols,
            bytes_accessed=2 * (total * depth + cols * depth + total * cols),
            transcendentals=0,
        ),
    )(xh.reshape(1).astype(jnp.int32), *arrays, *pieces)


def inputs_kernel(spans, core_ref, *refs):
    out_ref, chunks, wide_cols, sems = refs[-4:]
    copies = [
        pltpu.make_async_copy(ref, wide_cols.at[k], sems.at[len(spans) + k])
        for k, ref in enumerate(refs[len(spans) : len(spans) + 2])
    ]
    for k, (ref, (first, rows)) in enumerate(zip(refs[: len(spans)], spans)):
        source = ref.at[pl.ds(first, rows)]
        copies.append(pltpu.make_async_copy(source, chunks.at[k], sems.at[k]))
    for copy in copies:
        copy.start()
    for copy in copies:
        copy.wait()
    wide = [chunks[k].astype(F32) for k in range(len(spans))]
    depth = chunks.shape[2]
    quarters = wide_cols.shape[2] // depth
    totals = [0.0, 0.0]
    for q in range(quarters):
        rows = [
            w[first : first + 8]
            for w in wide
            for first in (q * 8, (quarters + q) * 8)
        ]
        heard = jnp.concatenate(rows).astype(BF16)
        for side in range(2):
            totals[side] += lax.dot_general(
                wide_cols[side, :, q * depth : (q + 1) * depth],
                heard,
                (((1,), (1,)), ((), ())),
                preferred_element_type=F32,
            )
    for side in range(2):
        out_ref[(core_ref[0] + side) % 2] = totals[side].astype(BF16)


def inputs(parts, own, other, core):
    arrays = [p[0] for p in parts]
    spans = [p[1:] for p in parts]
    rows, depth = spans[0][1], arrays[0].shape[1]
    tokens = rows * depth // own.shape[1] * len(parts)
    return pl.pallas_call(
        lambda *refs: inputs_kernel(spans, *refs),
        out_shape=jax.ShapeDtypeStruct((2, own.shape[0], tokens), BF16),
        in_specs=[pl.BlockSpec(memory_space=pltpu.SMEM)]
        + [pl.BlockSpec(memory_space=pltpu.HBM)] * (len(parts) + 2),
        out_specs=pl.BlockSpec(memory_space=pltpu.VMEM),
        scratch_shapes=[
            pltpu.VMEM((len(parts), rows, depth), BF16),
            pltpu.VMEM((2,) + own.shape, BF16),
            pltpu.SemaphoreType.DMA((len(parts) + 2,)),
        ],
        compiler_params=pltpu.CompilerParams(vmem_limit_bytes=60 << 20),
        cost_estimate=pl.CostEstimate(
            flops=4 * own.size * tokens,
            bytes_accessed=4 * own.size + 2 * len(parts) * rows * depth,
            transcendentals=0,
        ),
    )(core.reshape(1).astype(jnp.int32), *arrays, own, other)


def arrange_kernel(place_ref, near, below, above, two, out_ref):
    xh, z = place_ref[0], place_ref[1]
    for steps, ref, far in (
        (0, near, 0),
        (1, above, 0),
        (2, two, 1),
        (3, below, 1),
        (4, near, 1),
        (5, above, 1),
        (6, two, 0),
        (7, below, 0),
    ):
        for side in range(2):
            out_ref[(xh + side) % 2, (z + steps) % 8] = ref[far, side]


def arrange(place, *pieces):
    return pl.pallas_call(
        arrange_kernel,
        out_shape=jax.ShapeDtypeStruct((2, 8) + pieces[0].shape[2:], BF16),
        in_specs=[pl.BlockSpec(memory_space=pltpu.SMEM)]
        + [pl.BlockSpec(memory_space=pltpu.VMEM)] * 4,
        out_specs=pl.BlockSpec(memory_space=pltpu.VMEM),
        compiler_params=pltpu.CompilerParams(vmem_limit_bytes=16 << 20),
    )(place, *pieces)


def shards(acts, grads, basis_in, basis_out, tenant):
    tokens, hidden = grads.shape
    model = acts.shape[1]
    own_in, own_out = basis_in.shape[1], basis_out.shape[1]
    groups, planes = 8, 16
    rows = hidden // planes
    xh, z, core = (lax.axis_index(a) for a in ("xh", "z", "core"))

    in_cols = basis_in.T
    in_other = shift(in_cols, "core")
    acts_x = shift(acts, "xh")
    step = lambda i: ((i // 2 + 1 - 2 * (i % 2)) % 8) * 2 + i % 2
    turn = [(i, step(i)) for i in range(16)]
    over = [(i, step(i ^ 1)) for i in range(16)]
    ring = lambda x, way=turn: lax.ppermute(x, ("z", "core"), way)
    quarters = model // rows
    tall = lambda a: a.reshape(tokens, quarters, rows).transpose(1, 0, 2).reshape(-1, rows)
    own_acts = jnp.concatenate([tall(acts), tall(acts_x)])
    acts_1 = [ring(own_acts), ring(own_acts, over)]

    sent = grads.reshape(tokens, planes, rows).transpose(1, 0, 2)
    panel = lax.all_to_all(sent, ("xl", "y", "xh"), 0, 0).reshape(planes * tokens, rows)

    out_cols = basis_out.T
    keep = lax.dynamic_slice_in_dim(out_cols, xh * rows, rows, axis=1)
    give = lax.dynamic_slice_in_dim(out_cols, (1 - xh) * rows, rows, axis=1)
    panel, keep, give, *acts_1 = stage(panel, keep, give, *acts_1)
    size, extra = panel.shape[0], own_acts.shape[0]
    keep_c = shift(keep, "core")
    turned = ring(jnp.concatenate([panel, *acts_1]))
    crossed = ring(panel, over)
    got = [shift(give[: own_out // 2], "xh")]
    give, got[0], turned, crossed = stage(give, got[0], turned, crossed)
    block_2 = ring(jnp.concatenate([turned[:size], crossed, turned[size:]]))
    got.append(shift(give[own_out // 2 :], "xh"))
    got_c = [shift(got[0], "core")]
    got[1], block_2 = stage(got[1], block_2)
    got_c.append(shift(got[1], "core"))
    block_3 = ring(block_2[: 2 * size + extra])
    pieces = (keep, keep_c, *got, *got_c)
    parts = [(panel, 0), (turned, 0), (crossed, 0), (block_2, 0), (block_2, size)]
    out = product([(*p, size) for p in parts], pieces, xh, 40)
    out, block_3, in_cols, in_other, *pieces = stage(
        out, block_3, in_cols, in_other, *pieces
    )

    def home(out):
        out = out.reshape(planes, out.shape[2], 2 * own_out)
        return lax.all_to_all(out, ("xh", "xl", "y"), 0, 0)

    first = home(out)
    last = ring(block_3[:size])

    parts = [
        (own_acts, 0),
        *((a, 0) for a in acts_1),
        *((turned, size + k * extra) for k in range(2)),
        *((block_2, 2 * size + k * extra) for k in range(2)),
        (block_3, 2 * size),
    ]
    r = inputs([(*p, extra) for p in parts], in_cols, in_other, core).reshape(2 * own_in, 16 * tokens)
    r = jnp.concatenate([r, shift(r, "core")], axis=1)
    z_j, xh_j, row = np.unravel_index(np.arange(16 * tokens), (8, 2, tokens))
    apart = (z_j - z) % 8
    ran = jnp.where(apart % 4 == 0, core, (apart < 4).astype(core.dtype))
    away = jnp.minimum(apart, 8 - apart)
    slot = jnp.where(away == 0, 0, jnp.where(away == 4, 7, 2 * away - 1 + (ran ^ core)))
    source = (((ran ^ core) * 8 + slot) * 2 + (xh_j ^ xh)) * tokens + row
    pick = (jnp.arange(32 * tokens)[:, None] == source[None, :]).astype(BF16)
    r = jnp.dot(r, pick, preferred_element_type=F32).astype(BF16)

    far = shift(r, "z", 4)
    cross = shift(r, "xh")
    both = [((a, b), (1 - a, (b + 4) % 8)) for a in range(2) for b in range(8)]
    far_cross = lax.ppermute(
        r, ("xh", "z"), [(a * 8 + b, c * 8 + d) for (a, b), (c, d) in both]
    )
    parts = [(block_3, 0, size), (block_3, size, size), (last, 0, size)]
    out = product(parts, pieces, xh, 60)
    out, first, r, far, cross, far_cross = stage(out, first, r, far, cross, far_cross)
    second = home(out)

    quad = jnp.stack([jnp.stack([r, cross]), jnp.stack([far, far_cross])])
    below, above, two = shift(quad, "z", 1), shift(quad, "z", -1), shift(quad, "z", 2)
    added = lambda p: jnp.sum(p.astype(F32), axis=0).astype(BF16)
    below, above, two, first = stage(below, above, two, added(first))
    place = jnp.stack([xh, z]).astype(jnp.int32)
    r = arrange(place, quad, below, above, two).reshape(32 * own_in, 16 * tokens)
    r = jnp.concatenate([r, shift(r, "core")], axis=1)
    side, slot, half_x, row = np.unravel_index(
        np.arange(32 * tokens), (2, 8, 2, tokens)
    )
    ran = core ^ side
    steps = np.array([0, 1, 1, 2, 2, 3, 3, 4])[slot]
    from_core = ran ^ np.where(np.isin(slot, (0, 7)), 0, (slot - 1) % 2)
    z_of = (z + (2 * ran - 1) * steps) % 8
    source = (((from_core ^ core) * 8 + z_of) * 2 + half_x) * tokens + row
    pick = (jnp.arange(32 * tokens)[:, None] == source[None, :]).astype(BF16)
    rotated_in = jnp.dot(r, pick, preferred_element_type=F32).astype(BF16)

    mixed = jnp.concatenate([first, added(second)])
    left = jnp.concatenate([mixed[:, :own_out], shift(mixed[:, own_out:], "core")])

    corr = lax.dot_general(
        left, rotated_in, (((0,), (1,)), ((), ())), preferred_element_type=F32
    )
    square = (corr * corr).astype(BF16)
    parts = lax.all_to_all(
        square.reshape(groups, own_out // groups, square.shape[1]), GRP, 0, 0
    ).astype(F32)
    sums = jnp.stack(
        [
            jnp.sum(jnp.where((tenant == k)[:, None, None], parts, 0.0), axis=0)
            for k in range(TENANTS)
        ]
    )
    total = jnp.sum(sums, axis=0)
    seq_count = SEQ_GRP * groups
    scale = 1.0 / float((seq_count - seq_count // TENANTS) * 32 * tokens)
    return (total[None] - sums) * scale


def solution(mesh):
    fine = Mesh(mesh.devices.reshape(SIZES), AXES)
    tile = ("xh", "z", "core")
    return jax.shard_map(
        shards,
        mesh=fine,
        in_specs=(
            P(AXES, None),
            P(AXES, None),
            P(None, tile),
            P(GRP, tile),
            P(),
        ),
        out_specs=P(None, tile + GRP, None),
        check_vma=False,
    )
```

```python
import jax
import jax.numpy as jnp
import numpy as np
from jax import lax
from jax.experimental import pallas as pl
from jax.experimental.pallas import tpu as pltpu
from jax.sharding import Mesh, PartitionSpec as P

SEQ_GRP = 1
TENANTS = 2
AXES = ("xl", "y", "xh", "z", "core")
SIZES = (2, 4, 2, 8, 2)
GRP = ("xl", "y")
BF16, F32 = jnp.bfloat16, jnp.float32


def shift(x, axis, step=1):
    count = SIZES[AXES.index(axis)]
    return lax.ppermute(x, axis, [(i, (i + step) % count) for i in range(count)])


def stage(*arrays):
    return lax.optimization_barrier(arrays)


def ordered(x, other, axis):
    first = lax.axis_index(axis) == 0
    return jnp.concatenate([jnp.where(first, x, other), jnp.where(first, other, x)])


def rows_dot(a, b):
    return lax.dot_general(
        a, b, (((1,), (1,)), ((), ())), preferred_element_type=F32
    ).astype(BF16)


def product_kernel(spans, xh_ref, *refs):
    out_ref, left, right, ready_out, sems = refs[-5:]
    sources, pieces = refs[: len(spans)], refs[len(spans) : -5]
    copies, row = [], 0
    for k, (ref, (first, rows)) in enumerate(zip(sources, spans)):
        copies.append(
            pltpu.make_async_copy(
                ref.at[pl.ds(first, rows)], left.at[pl.ds(row, rows)], sems.at[k]
            )
        )
        row += rows
    row = 0
    for k, ref in enumerate(pieces, len(spans)):
        place = right.at[pl.ds(row, ref.shape[0])]
        copies.append(pltpu.make_async_copy(ref, place, sems.at[k]))
        row += ref.shape[0]
    for copy in copies:
        copy.start()
    groups, cols = out_ref.shape[1], out_ref.shape[3]
    step = 16
    waited, sent = 0, []
    for half, ready in enumerate((len(spans) + 2, len(copies))):
        for copy in copies[waited:ready]:
            copy.wait()
        waited = ready
        out = lax.dot_general(
            left[...],
            right[half * cols : (half + 1) * cols],
            (((1,), (1,)), ((), ())),
            preferred_element_type=F32,
        ).astype(BF16)
        side = (xh_ref[0] + half) % 2
        for slot in range(left.shape[0] // (groups * step)):
            for group in range(groups):
                row = (slot * groups + group) * step
                ready_out[half, group, slot * step : (slot + 1) * step] = out[
                    row : row + step
                ]
        send = pltpu.make_async_copy(
            ready_out.at[half], out_ref.at[side], sems.at[len(copies) + half]
        )
        send.start()
        sent.append(send)
    for send in sent:
        send.wait()


def product(parts, pieces, xh, grant):
    arrays = [p[0] for p in parts]
    depth = arrays[0].shape[1]
    total = sum(p[2] for p in parts)
    cols = sum(p.shape[0] for p in pieces)
    spans = [p[1:] for p in parts]
    return pl.pallas_call(
        lambda *refs: product_kernel(spans, *refs),
        out_shape=jax.ShapeDtypeStruct((2, 8, total // 8, cols // 2), BF16),
        in_specs=[pl.BlockSpec(memory_space=pltpu.SMEM)]
        + [pl.BlockSpec(memory_space=pl.ANY)] * (len(parts) + len(pieces)),
        out_specs=pl.BlockSpec(memory_space=pltpu.HBM),
        scratch_shapes=[
            pltpu.VMEM((total, depth), BF16),
            pltpu.VMEM((cols, depth), BF16),
            pltpu.VMEM((2, 8, total // 8, cols // 2), BF16),
            pltpu.SemaphoreType.DMA((len(parts) + len(pieces) + 2,)),
        ],
        compiler_params=pltpu.CompilerParams(vmem_limit_bytes=grant << 20),
        cost_estimate=pl.CostEstimate(
            flops=2 * total * depth * cols,
            bytes_accessed=2 * (total * depth + cols * depth + total * cols),
            transcendentals=0,
        ),
    )(xh.reshape(1).astype(jnp.int32), *arrays, *pieces)


def inputs_kernel(spans, core_ref, *refs):
    out_ref, chunks, wide_cols, sems = refs[-4:]
    copies = [
        pltpu.make_async_copy(ref, wide_cols.at[k], sems.at[len(spans) + k])
        for k, ref in enumerate(refs[len(spans) : len(spans) + 2])
    ]
    for k, (ref, (first, rows)) in enumerate(zip(refs[: len(spans)], spans)):
        source = ref.at[pl.ds(first, rows)]
        copies.append(pltpu.make_async_copy(source, chunks.at[k], sems.at[k]))
    for copy in copies:
        copy.start()
    for copy in copies:
        copy.wait()
    wide = [chunks[k].astype(F32) for k in range(len(spans))]
    depth = chunks.shape[2]
    quarters = wide_cols.shape[2] // depth
    totals = [0.0, 0.0]
    for q in range(quarters):
        rows = [
            w[first : first + 8]
            for w in wide
            for first in (q * 8, (quarters + q) * 8)
        ]
        heard = jnp.concatenate(rows).astype(BF16)
        for side in range(2):
            totals[side] += lax.dot_general(
                wide_cols[side, :, q * depth : (q + 1) * depth],
                heard,
                (((1,), (1,)), ((), ())),
                preferred_element_type=F32,
            )
    for side in range(2):
        out_ref[(core_ref[0] + side) % 2] = totals[side].astype(BF16)


def inputs(parts, own, other, core):
    arrays = [p[0] for p in parts]
    spans = [p[1:] for p in parts]
    rows, depth = spans[0][1], arrays[0].shape[1]
    tokens = rows * depth // own.shape[1] * len(parts)
    return pl.pallas_call(
        lambda *refs: inputs_kernel(spans, *refs),
        out_shape=jax.ShapeDtypeStruct((2, own.shape[0], tokens), BF16),
        in_specs=[pl.BlockSpec(memory_space=pltpu.SMEM)]
        + [pl.BlockSpec(memory_space=pltpu.HBM)] * (len(parts) + 2),
        out_specs=pl.BlockSpec(memory_space=pltpu.VMEM),
        scratch_shapes=[
            pltpu.VMEM((len(parts), rows, depth), BF16),
            pltpu.VMEM((2,) + own.shape, BF16),
            pltpu.SemaphoreType.DMA((len(parts) + 2,)),
        ],
        compiler_params=pltpu.CompilerParams(vmem_limit_bytes=60 << 20),
        cost_estimate=pl.CostEstimate(
            flops=4 * own.size * tokens,
            bytes_accessed=4 * own.size + 2 * len(parts) * rows * depth,
            transcendentals=0,
        ),
    )(core.reshape(1).astype(jnp.int32), *arrays, own, other)


def arrange_kernel(place_ref, near, below, above, two, out_ref):
    xh, z = place_ref[0], place_ref[1]
    for steps, ref, far in (
        (0, near, 0),
        (1, above, 0),
        (2, two, 1),
        (3, below, 1),
        (4, near, 1),
        (5, above, 1),
        (6, two, 0),
        (7, below, 0),
    ):
        for side in range(2):
            out_ref[(xh + side) % 2, (z + steps) % 8] = ref[far, side]


def arrange(place, *pieces):
    return pl.pallas_call(
        arrange_kernel,
        out_shape=jax.ShapeDtypeStruct((2, 8) + pieces[0].shape[2:], BF16),
        in_specs=[pl.BlockSpec(memory_space=pltpu.SMEM)]
        + [pl.BlockSpec(memory_space=pltpu.VMEM)] * 4,
        out_specs=pl.BlockSpec(memory_space=pltpu.VMEM),
        compiler_params=pltpu.CompilerParams(vmem_limit_bytes=16 << 20),
    )(place, *pieces)


def shards(acts, grads, basis_in, basis_out, tenant):
    tokens, hidden = grads.shape
    model = acts.shape[1]
    own_in, own_out = basis_in.shape[1], basis_out.shape[1]
    groups, planes = 8, 16
    rows = hidden // planes
    xh, z, core = (lax.axis_index(a) for a in ("xh", "z", "core"))

    in_cols = basis_in.T
    in_other = shift(in_cols, "core")
    acts_x = shift(acts, "xh")
    step = lambda i: ((i // 2 + 1 - 2 * (i % 2)) % 8) * 2 + i % 2
    turn = [(i, step(i)) for i in range(16)]
    over = [(i, step(i ^ 1)) for i in range(16)]
    ring = lambda x, way=turn: lax.ppermute(x, ("z", "core"), way)
    quarters = model // rows
    tall = lambda a: a.reshape(tokens, quarters, rows).transpose(1, 0, 2).reshape(-1, rows)
    own_acts = jnp.concatenate([tall(acts), tall(acts_x)])
    acts_1 = [ring(own_acts), ring(own_acts, over)]

    sent = grads.reshape(tokens, planes, rows).transpose(1, 0, 2)
    panel = lax.all_to_all(sent, ("xl", "y", "xh"), 0, 0).reshape(planes * tokens, rows)

    out_cols = basis_out.T
    keep = lax.dynamic_slice_in_dim(out_cols, xh * rows, rows, axis=1)
    give = lax.dynamic_slice_in_dim(out_cols, (1 - xh) * rows, rows, axis=1)
    panel, keep, give, *acts_1 = stage(panel, keep, give, *acts_1)
    size, extra = panel.shape[0], own_acts.shape[0]
    keep_c = shift(keep, "core")
    turned = ring(jnp.concatenate([panel, *acts_1]))
    crossed = ring(panel, over)
    got = [shift(give[: own_out // 2], "xh")]
    give, got[0], turned, crossed = stage(give, got[0], turned, crossed)
    block_2 = ring(jnp.concatenate([turned[:size], crossed, turned[size:]]))
    got.append(shift(give[own_out // 2 :], "xh"))
    got_c = [shift(got[0], "core")]
    got[1], block_2 = stage(got[1], block_2)
    got_c.append(shift(got[1], "core"))
    block_3 = ring(block_2[: 2 * size + extra])
    pieces = (keep, keep_c, *got, *got_c)
    parts = [(panel, 0), (turned, 0), (crossed, 0), (block_2, 0), (block_2, size)]
    out = product([(*p, size) for p in parts], pieces, xh, 40)
    out, block_3, in_cols, in_other, *pieces = stage(
        out, block_3, in_cols, in_other, *pieces
    )

    def home(out):
        out = out.reshape(planes, out.shape[2], 2 * own_out)
        return lax.all_to_all(out, ("xh", "xl", "y"), 0, 0)

    first = home(out)
    last = ring(block_3[:size])

    parts = [
        (own_acts, 0),
        *((a, 0) for a in acts_1),
        *((turned, size + k * extra) for k in range(2)),
        *((block_2, 2 * size + k * extra) for k in range(2)),
        (block_3, 2 * size),
    ]
    r = inputs([(*p, extra) for p in parts], in_cols, in_other, core).reshape(2 * own_in, 16 * tokens)
    r = jnp.concatenate([r, shift(r, "core")], axis=1)
    z_j, xh_j, row = np.unravel_index(np.arange(16 * tokens), (8, 2, tokens))
    apart = (z_j - z) % 8
    ran = jnp.where(apart % 4 == 0, core, (apart < 4).astype(core.dtype))
    away = jnp.minimum(apart, 8 - apart)
    slot = jnp.where(away == 0, 0, jnp.where(away == 4, 7, 2 * away - 1 + (ran ^ core)))
    source = (((ran ^ core) * 8 + slot) * 2 + (xh_j ^ xh)) * tokens + row
    pick = (jnp.arange(32 * tokens)[:, None] == source[None, :]).astype(BF16)
    r = jnp.dot(r, pick, preferred_element_type=F32).astype(BF16)

    both = [((a, b), (1 - a, (b + 4) % 8)) for a in range(2) for b in range(8)]
    far_cross = lax.ppermute(
        r, ("xh", "z"), [(a * 8 + b, c * 8 + d) for (a, b), (c, d) in both]
    )
    cross = shift(r, "xh")
    far = shift(r, "z", 4)
    parts = [(block_3, 0, size), (block_3, size, size), (last, 0, size)]
    out = product(parts, pieces, xh, 60)
    out, first, r, far_cross, cross, far = stage(out, first, r, far_cross, cross, far)
    second = home(out)

    quad = jnp.stack([jnp.stack([r, cross]), jnp.stack([far, far_cross])])
    two = shift(quad, "z", 2)
    below, above = shift(quad, "z", 1), shift(quad, "z", -1)
    added = lambda p: jnp.sum(p.astype(F32), axis=0).astype(BF16)
    two, below, above, first = stage(two, below, above, added(first))
    place = jnp.stack([xh, z]).astype(jnp.int32)
    r = arrange(place, quad, below, above, two).reshape(32 * own_in, 16 * tokens)
    r = jnp.concatenate([r, shift(r, "core")], axis=1)
    side, slot, half_x, row = np.unravel_index(
        np.arange(32 * tokens), (2, 8, 2, tokens)
    )
    ran = core ^ side
    steps = np.array([0, 1, 1, 2, 2, 3, 3, 4])[slot]
    from_core = ran ^ np.where(np.isin(slot, (0, 7)), 0, (slot - 1) % 2)
    z_of = (z + (2 * ran - 1) * steps) % 8
    source = (((from_core ^ core) * 8 + z_of) * 2 + half_x) * tokens + row
    pick = (jnp.arange(32 * tokens)[:, None] == source[None, :]).astype(BF16)
    rotated_in = jnp.dot(r, pick, preferred_element_type=F32).astype(BF16)

    mixed = jnp.concatenate([first, added(second)])
    left = jnp.concatenate([mixed[:, :own_out], shift(mixed[:, own_out:], "core")])

    corr = lax.dot_general(
        left, rotated_in, (((0,), (1,)), ((), ())), preferred_element_type=F32
    )
    square = (corr * corr).astype(BF16)
    parts = lax.all_to_all(
        square.reshape(groups, own_out // groups, square.shape[1]), GRP, 0, 0
    ).astype(F32)
    sums = jnp.stack(
        [
            jnp.sum(jnp.where((tenant == k)[:, None, None], parts, 0.0), axis=0)
            for k in range(TENANTS)
        ]
    )
    total = jnp.sum(sums, axis=0)
    seq_count = SEQ_GRP * groups
    scale = 1.0 / float((seq_count - seq_count // TENANTS) * 32 * tokens)
    return (total[None] - sums) * scale


def solution(mesh):
    fine = Mesh(mesh.devices.reshape(SIZES), AXES)
    tile = ("xh", "z", "core")
    return jax.shard_map(
        shards,
        mesh=fine,
        in_specs=(
            P(AXES, None),
            P(AXES, None),
            P(None, tile),
            P(GRP, tile),
            P(),
        ),
        out_specs=P(None, tile + GRP, None),
        check_vma=False,
    )
```

```python
import jax
import jax.numpy as jnp
import numpy as np
from jax import lax
from jax.experimental import pallas as pl
from jax.experimental.pallas import tpu as pltpu
from jax.sharding import Mesh, PartitionSpec as P

SEQ_GRP = 1
TENANTS = 2
AXES = ("xl", "y", "xh", "z", "core")
SIZES = (2, 4, 2, 8, 2)
GRP = ("xl", "y")
BF16, F32 = jnp.bfloat16, jnp.float32


def shift(x, axis, step=1):
    count = SIZES[AXES.index(axis)]
    return lax.ppermute(x, axis, [(i, (i + step) % count) for i in range(count)])


def stage(*arrays):
    return lax.optimization_barrier(arrays)


def ordered(x, other, axis):
    first = lax.axis_index(axis) == 0
    return jnp.concatenate([jnp.where(first, x, other), jnp.where(first, other, x)])


def rows_dot(a, b):
    return lax.dot_general(
        a, b, (((1,), (1,)), ((), ())), preferred_element_type=F32
    ).astype(BF16)


def product_kernel(spans, xh_ref, *refs):
    out_ref, left, right, ready_out, sems = refs[-5:]
    sources, pieces = refs[: len(spans)], refs[len(spans) : -5]
    copies, row = [], 0
    for k, (ref, (first, rows)) in enumerate(zip(sources, spans)):
        copies.append(
            pltpu.make_async_copy(
                ref.at[pl.ds(first, rows)], left.at[pl.ds(row, rows)], sems.at[k]
            )
        )
        row += rows
    row = 0
    for k, ref in enumerate(pieces, len(spans)):
        place = right.at[pl.ds(row, ref.shape[0])]
        copies.append(pltpu.make_async_copy(ref, place, sems.at[k]))
        row += ref.shape[0]
    for copy in copies:
        copy.start()
    groups, cols = out_ref.shape[1], out_ref.shape[3]
    step = 16
    waited, sent = 0, []
    for half, ready in enumerate((len(spans) + 2, len(copies))):
        for copy in copies[waited:ready]:
            copy.wait()
        waited = ready
        out = lax.dot_general(
            left[...],
            right[half * cols : (half + 1) * cols],
            (((1,), (1,)), ((), ())),
            preferred_element_type=F32,
        ).astype(BF16)
        side = (xh_ref[0] + half) % 2
        for slot in range(left.shape[0] // (groups * step)):
            for group in range(groups):
                row = (slot * groups + group) * step
                ready_out[half, group, slot * step : (slot + 1) * step] = out[
                    row : row + step
                ]
        send = pltpu.make_async_copy(
            ready_out.at[half], out_ref.at[side], sems.at[len(copies) + half]
        )
        send.start()
        sent.append(send)
    for send in sent:
        send.wait()


def product(parts, pieces, xh, grant):
    arrays = [p[0] for p in parts]
    depth = arrays[0].shape[1]
    total = sum(p[2] for p in parts)
    cols = sum(p.shape[0] for p in pieces)
    spans = [p[1:] for p in parts]
    return pl.pallas_call(
        lambda *refs: product_kernel(spans, *refs),
        out_shape=jax.ShapeDtypeStruct((2, 8, total // 8, cols // 2), BF16),
        in_specs=[pl.BlockSpec(memory_space=pltpu.SMEM)]
        + [pl.BlockSpec(memory_space=pl.ANY)] * (len(parts) + len(pieces)),
        out_specs=pl.BlockSpec(memory_space=pltpu.HBM),
        scratch_shapes=[
            pltpu.VMEM((total, depth), BF16),
            pltpu.VMEM((cols, depth), BF16),
            pltpu.VMEM((2, 8, total // 8, cols // 2), BF16),
            pltpu.SemaphoreType.DMA((len(parts) + len(pieces) + 2,)),
        ],
        compiler_params=pltpu.CompilerParams(vmem_limit_bytes=grant << 20),
        cost_estimate=pl.CostEstimate(
            flops=2 * total * depth * cols,
            bytes_accessed=2 * (total * depth + cols * depth + total * cols),
            transcendentals=0,
        ),
    )(xh.reshape(1).astype(jnp.int32), *arrays, *pieces)


def inputs_kernel(spans, core_ref, *refs):
    out_ref, chunks, wide_cols, sems = refs[-4:]
    copies = [
        pltpu.make_async_copy(ref, wide_cols.at[k], sems.at[len(spans) + k])
        for k, ref in enumerate(refs[len(spans) : len(spans) + 2])
    ]
    for k, (ref, (first, rows)) in enumerate(zip(refs[: len(spans)], spans)):
        source = ref.at[pl.ds(first, rows)]
        copies.append(pltpu.make_async_copy(source, chunks.at[k], sems.at[k]))
    for copy in copies:
        copy.start()
    for copy in copies:
        copy.wait()
    wide = [chunks[k].astype(F32) for k in range(len(spans))]
    depth = chunks.shape[2]
    quarters = wide_cols.shape[2] // depth
    totals = [0.0, 0.0]
    for q in range(quarters):
        rows = [
            w[first : first + 8]
            for w in wide
            for first in (q * 8, (quarters + q) * 8)
        ]
        heard = jnp.concatenate(rows).astype(BF16)
        for side in range(2):
            totals[side] += lax.dot_general(
                wide_cols[side, :, q * depth : (q + 1) * depth],
                heard,
                (((1,), (1,)), ((), ())),
                preferred_element_type=F32,
            )
    for side in range(2):
        out_ref[(core_ref[0] + side) % 2] = totals[side].astype(BF16)


def inputs(parts, own, other, core):
    arrays = [p[0] for p in parts]
    spans = [p[1:] for p in parts]
    rows, depth = spans[0][1], arrays[0].shape[1]
    tokens = rows * depth // own.shape[1] * len(parts)
    return pl.pallas_call(
        lambda *refs: inputs_kernel(spans, *refs),
        out_shape=jax.ShapeDtypeStruct((2, own.shape[0], tokens), BF16),
        in_specs=[pl.BlockSpec(memory_space=pltpu.SMEM)]
        + [pl.BlockSpec(memory_space=pltpu.HBM)] * (len(parts) + 2),
        out_specs=pl.BlockSpec(memory_space=pltpu.VMEM),
        scratch_shapes=[
            pltpu.VMEM((len(parts), rows, depth), BF16),
            pltpu.VMEM((2,) + own.shape, BF16),
            pltpu.SemaphoreType.DMA((len(parts) + 2,)),
        ],
        compiler_params=pltpu.CompilerParams(vmem_limit_bytes=60 << 20),
        cost_estimate=pl.CostEstimate(
            flops=4 * own.size * tokens,
            bytes_accessed=4 * own.size + 2 * len(parts) * rows * depth,
            transcendentals=0,
        ),
    )(core.reshape(1).astype(jnp.int32), *arrays, own, other)


def arrange_kernel(place_ref, near, below, above, two, out_ref):
    xh, z = place_ref[0], place_ref[1]
    for steps, ref, far in (
        (0, near, 0),
        (1, above, 0),
        (2, two, 1),
        (3, below, 1),
        (4, near, 1),
        (5, above, 1),
        (6, two, 0),
        (7, below, 0),
    ):
        for side in range(2):
            out_ref[(xh + side) % 2, (z + steps) % 8] = ref[far, side]


def arrange(place, *pieces):
    return pl.pallas_call(
        arrange_kernel,
        out_shape=jax.ShapeDtypeStruct((2, 8) + pieces[0].shape[2:], BF16),
        in_specs=[pl.BlockSpec(memory_space=pltpu.SMEM)]
        + [pl.BlockSpec(memory_space=pltpu.VMEM)] * 4,
        out_specs=pl.BlockSpec(memory_space=pltpu.VMEM),
        compiler_params=pltpu.CompilerParams(vmem_limit_bytes=16 << 20),
    )(place, *pieces)


def shards(acts, grads, basis_in, basis_out, tenant):
    tokens, hidden = grads.shape
    model = acts.shape[1]
    own_in, own_out = basis_in.shape[1], basis_out.shape[1]
    groups, planes = 8, 16
    rows = hidden // planes
    xh, z, core = (lax.axis_index(a) for a in ("xh", "z", "core"))

    in_cols = basis_in.T
    in_other = shift(in_cols, "core")
    acts_x = shift(acts, "xh")
    step = lambda i: ((i // 2 + 1 - 2 * (i % 2)) % 8) * 2 + i % 2
    turn = [(i, step(i)) for i in range(16)]
    over = [(i, step(i ^ 1)) for i in range(16)]
    ring = lambda x, way=turn: lax.ppermute(x, ("z", "core"), way)
    quarters = model // rows
    tall = lambda a: a.reshape(tokens, quarters, rows).transpose(1, 0, 2).reshape(-1, rows)
    own_acts = jnp.concatenate([tall(acts), tall(acts_x)])
    acts_1 = [ring(own_acts), ring(own_acts, over)]

    sent = grads.reshape(tokens, planes, rows).transpose(1, 0, 2)
    panel = lax.all_to_all(sent, ("xl", "y", "xh"), 0, 0).reshape(planes * tokens, rows)

    out_cols = basis_out.T
    keep = lax.dynamic_slice_in_dim(out_cols, xh * rows, rows, axis=1)
    give = lax.dynamic_slice_in_dim(out_cols, (1 - xh) * rows, rows, axis=1)
    panel, keep, give, *acts_1 = stage(panel, keep, give, *acts_1)
    size, extra = panel.shape[0], own_acts.shape[0]
    keep_c = shift(keep, "core")
    turned = ring(jnp.concatenate([panel, *acts_1]))
    crossed = ring(panel, over)
    got = [shift(give[: own_out // 2], "xh")]
    give, got[0], turned, crossed = stage(give, got[0], turned, crossed)
    block_2 = ring(jnp.concatenate([turned[:size], crossed, turned[size:]]))
    got.append(shift(give[own_out // 2 :], "xh"))
    got_c = [shift(got[0], "core")]
    got[1], block_2 = stage(got[1], block_2)
    got_c.append(shift(got[1], "core"))
    block_3 = ring(block_2[: 2 * size + extra])
    pieces = (keep, keep_c, *got, *got_c)
    parts = [(panel, 0), (turned, 0), (crossed, 0), (block_2, 0), (block_2, size)]
    out = product([(*p, size) for p in parts], pieces, xh, 40)
    out, block_3, in_cols, in_other, *pieces = stage(
        out, block_3, in_cols, in_other, *pieces
    )

    def home(out):
        out = out.reshape(planes, out.shape[2], 2 * own_out)
        return lax.all_to_all(out, ("xh", "xl", "y"), 0, 0)

    first = home(out)

    parts = [
        (own_acts, 0),
        *((a, 0) for a in acts_1),
        *((turned, size + k * extra) for k in range(2)),
        *((block_2, 2 * size + k * extra) for k in range(2)),
        (block_3, 2 * size),
    ]
    r = inputs([(*p, extra) for p in parts], in_cols, in_other, core)
    r, end = stage(r, block_3)
    last = ring(end[:size])
    r = r.reshape(2 * own_in, 16 * tokens)
    r = jnp.concatenate([r, shift(r, "core")], axis=1)
    z_j, xh_j, row = np.unravel_index(np.arange(16 * tokens), (8, 2, tokens))
    apart = (z_j - z) % 8
    ran = jnp.where(apart % 4 == 0, core, (apart < 4).astype(core.dtype))
    away = jnp.minimum(apart, 8 - apart)
    slot = jnp.where(away == 0, 0, jnp.where(away == 4, 7, 2 * away - 1 + (ran ^ core)))
    source = (((ran ^ core) * 8 + slot) * 2 + (xh_j ^ xh)) * tokens + row
    pick = (jnp.arange(32 * tokens)[:, None] == source[None, :]).astype(BF16)
    r = jnp.dot(r, pick, preferred_element_type=F32).astype(BF16)

    both = [((a, b), (1 - a, (b + 4) % 8)) for a in range(2) for b in range(8)]
    far_cross = lax.ppermute(
        r, ("xh", "z"), [(a * 8 + b, c * 8 + d) for (a, b), (c, d) in both]
    )
    cross = shift(r, "xh")
    far = shift(r, "z", 4)
    parts = [(block_3, 0, size), (block_3, size, size), (last, 0, size)]
    out = product(parts, pieces, xh, 60)
    out, first, r, far_cross, cross, far = stage(out, first, r, far_cross, cross, far)
    second = home(out)

    quad = jnp.stack([jnp.stack([r, cross]), jnp.stack([far, far_cross])])
    two = shift(quad, "z", 2)
    below, above = shift(quad, "z", 1), shift(quad, "z", -1)
    added = lambda p: jnp.sum(p.astype(F32), axis=0).astype(BF16)
    two, below, above, first = stage(two, below, above, added(first))
    place = jnp.stack([xh, z]).astype(jnp.int32)
    r = arrange(place, quad, below, above, two).reshape(32 * own_in, 16 * tokens)
    r = jnp.concatenate([r, shift(r, "core")], axis=1)
    side, slot, half_x, row = np.unravel_index(
        np.arange(32 * tokens), (2, 8, 2, tokens)
    )
    ran = core ^ side
    steps = np.array([0, 1, 1, 2, 2, 3, 3, 4])[slot]
    from_core = ran ^ np.where(np.isin(slot, (0, 7)), 0, (slot - 1) % 2)
    z_of = (z + (2 * ran - 1) * steps) % 8
    source = (((from_core ^ core) * 8 + z_of) * 2 + half_x) * tokens + row
    pick = (jnp.arange(32 * tokens)[:, None] == source[None, :]).astype(BF16)
    rotated_in = jnp.dot(r, pick, preferred_element_type=F32).astype(BF16)

    mixed = jnp.concatenate([first, added(second)])
    left = jnp.concatenate([mixed[:, :own_out], shift(mixed[:, own_out:], "core")])

    corr = lax.dot_general(
        left, rotated_in, (((0,), (1,)), ((), ())), preferred_element_type=F32
    )
    square = (corr * corr).astype(BF16)
    parts = lax.all_to_all(
        square.reshape(groups, own_out // groups, square.shape[1]), GRP, 0, 0
    ).astype(F32)
    sums = jnp.stack(
        [
            jnp.sum(jnp.where((tenant == k)[:, None, None], parts, 0.0), axis=0)
            for k in range(TENANTS)
        ]
    )
    total = jnp.sum(sums, axis=0)
    seq_count = SEQ_GRP * groups
    scale = 1.0 / float((seq_count - seq_count // TENANTS) * 32 * tokens)
    return (total[None] - sums) * scale


def solution(mesh):
    fine = Mesh(mesh.devices.reshape(SIZES), AXES)
    tile = ("xh", "z", "core")
    return jax.shard_map(
        shards,
        mesh=fine,
        in_specs=(
            P(AXES, None),
            P(AXES, None),
            P(None, tile),
            P(GRP, tile),
            P(),
        ),
        out_specs=P(None, tile + GRP, None),
        check_vma=False,
    )
```
